32 devices in a mesh: wave: 8 (over z, x), band: 4 (over y, core).
Axes of the slice: x: 2, y: 2, z: 4, core: 2. Of those that a mesh axis runs over, the one named last changes fastest.
Arguments:
- spectral: bfloat16 [1920, 2, 128, 1280], P('wave', None, 'band'), may hold values from -0.0059814453 to 0.0059814453
- legendre: bfloat16 [1920, 8, 1280], P('wave'), may hold values from -4 to 4
- slot_wave: int32 [1920], replicated, may hold values from 0 to 1280, as said below
- lat_points: int32 [8], P('wave'), may hold values from 20 to 5136, as said below
- level_mix: float32 [32, 32], replicated, may hold values from -1 to 1
- grid_scale: float32 [8, 5632], P('wave', 'band'), may hold values from 0.5 to 2
- gauss_w: float32 [8], replicated, may hold values from 2 to 8
Outputs:
- grid_out: float32 [128, 8, 5632], P(None, 'wave', 'band')
- spec_out: bfloat16 [1920, 2, 128, 1280], P('wave', None, 'band')
The draws below stay inside these ranges and needn't reach their ends.
Inputs may be any that keep to these rules, and one draw needn't show every extreme that they name: `slot_wave`: every wavenumber 0 to 1279 is held by exactly one slot; all other slots hold 1280; some index of wave has all 240 of its slots holding wavenumbers. `lat_points`: each value is 20 + 4 i for a latitude row i from 0 to 1279; some latitude has 5136 points.
All inputs are finite; a program needn't handle non-finite values.
Results may differ from the reference program's by a relative error of at most 0.0062.
Values may be sent and summed in bfloat16 or wider, within the bound.
A program may use at most 192 MiB of HBM per device.

```python
import math
import jax
import jax.numpy as jnp
from jax import lax

M = 1280
NLEV = 32
FIELDS = 128
LAT = 8
MSLOT = 240
SLOTS = 1920
LONS = 5632


def draw_slot_wave(key, part):
    key_full = jax.random.fold_in(key, 11)
    key_rank = jax.random.fold_in(key, 12)
    key_wave = jax.random.fold_in(key, 13)
    full_device = jax.random.randint(key_full, (), 0, SLOTS // MSLOT)
    slot_index = jnp.arange(SLOTS, dtype=jnp.int32)
    in_full = slot_index // MSLOT == full_device
    random_rank = jax.random.permutation(key_rank, SLOTS).astype(jnp.int32)
    score = jnp.where(in_full, -1, random_rank)
    order = jnp.argsort(score, stable=True).astype(jnp.int32)
    position = jnp.zeros((SLOTS,), jnp.int32).at[order].set(slot_index)
    wave_perm = jax.random.permutation(key_wave, M).astype(jnp.int32)
    live_slot = position < M
    picked = wave_perm[jnp.minimum(position, M - 1)]
    return jnp.where(live_slot, picked, M).astype(jnp.int32)


def draw_lat_points(key, part):
    key_rows = jax.random.fold_in(key, 21)
    key_spot = jax.random.fold_in(key, 22)
    lat_rows = jax.random.randint(key_rows, (LAT,), 0, M)
    spot = jax.random.randint(key_spot, (), 0, LAT)
    lat_rows = jnp.where(jnp.arange(LAT) == spot, M - 1, lat_rows)
    return (20 + 4 * lat_rows).astype(jnp.int32)


def block_levels(rng, extent, cuts, least, largest):
    def one(dim, parts):
        steps = jax.random.uniform(jax.random.fold_in(jax.random.fold_in(rng, 6), dim), (parts,), jnp.float32, least / len(cuts), largest / len(cuts))
        return jnp.repeat(jnp.exp(steps), extent[dim] // parts).reshape((-1,) + (1,) * (len(extent) - dim - 1))

    level = one(*cuts[0])
    for cut in cuts[1:]:
        level = level * one(*cut)
    return level


def gaussian(rng, shape, scale, bound, pieces=(), kind=jnp.bfloat16):
    drawn = jax.random.normal(rng, shape, jnp.float32) * scale
    if len(pieces) > 0:
        drawn = block_levels(rng, shape, pieces, -0.22, 0.18) * drawn
    return jnp.clip(drawn, min=-bound, max=bound).astype(kind)


def setup_inputs(seed: int = 0) -> dict:
    seeds = jax.random.split(jax.random.key(seed), 8)
    spectral = gaussian(seeds[0], (SLOTS, 2, FIELDS, M), 0.001, 0.0059814453, ((0, 8), (2, 4)))
    legendre = gaussian(seeds[1], (SLOTS, LAT, M), 1.0, 4.0, ((0, 8),))
    slot_wave = draw_slot_wave(jax.random.fold_in(seeds[7], 71), 0)
    lat_points = draw_lat_points(jax.random.fold_in(seeds[7], 71), 0)
    level_mix = gaussian(seeds[4], (NLEV, NLEV), NLEV ** -0.5, 1.0, (), jnp.float32)
    grid_scale = jnp.clip(jnp.exp(math.log(2.0) - 1.3862944 * jax.random.uniform(seeds[5], (LAT, LONS), jnp.float32) ** block_levels(seeds[5], (LAT, LONS), ((0, 8), (1, 4)), -0.2, 0.2)), 0.5, 2.0)
    gauss_w = jnp.clip(jnp.exp(jax.random.uniform(seeds[6], (LAT,), jnp.float32, math.log(2.0), math.log(8.0))), 2.0, 8.0)
    return dict(spectral=spectral, legendre=legendre, slot_wave=slot_wave, lat_points=lat_points, level_mix=level_mix, grid_scale=grid_scale, gauss_w=gauss_w)


TWO_PI = 2.0 * math.pi


def trig_table(wave_ids, points, lon_first, lon_width):
    lon_index = lon_first + jnp.arange(lon_width, dtype=jnp.int32)
    turn_index = (wave_ids[None, :, None] * lon_index[None, None, :]) % points[:, None, None]
    angle_rad = turn_index.astype(jnp.float32) * (TWO_PI / points.astype(jnp.float32))[:, None, None]
    return jnp.stack([jnp.cos(angle_rad), jnp.sin(angle_rad)], axis=2)


def valid_waves(wave_ids, points):
    return ((wave_ids[None, :] < M) & (2 * wave_ids[None, :] < points[:, None])).astype(jnp.float32)


def lon_mask(points, lon_first, lon_width):
    lon_index = lon_first + jnp.arange(lon_width, dtype=jnp.int32)
    return (lon_index[None, :] < points[:, None]).astype(jnp.float32)


def inverse_terms(four_coef, wave_ids, points, lon_first, lon_width):
    valid_wave = valid_waves(wave_ids, points)
    doubled = jnp.where(wave_ids == 0, 1.0, 2.0).astype(jnp.float32)
    sign_pair = jnp.array([1.0, -1.0], jnp.float32)
    factor = (valid_wave * doubled[None, :])[:, :, None] * sign_pair
    weighted = four_coef.astype(jnp.float32) * jnp.transpose(factor, (1, 2, 0))[:, :, None, :]
    trig_tab = trig_table(wave_ids, points, lon_first, lon_width)
    grid_rows = jnp.einsum('scfa,ascj->faj', weighted, trig_tab, precision=lax.Precision.HIGHEST)
    return grid_rows * lon_mask(points, lon_first, lon_width)[None]


def direct_terms(grid_rows, wave_ids, points, lon_first, lon_width):
    valid_wave = valid_waves(wave_ids, points)
    sign_pair = jnp.array([1.0, -1.0], jnp.float32)
    trig_tab = trig_table(wave_ids, points, lon_first, lon_width)
    masked_rows = grid_rows * lon_mask(points, lon_first, lon_width)[None]
    summed = jnp.einsum('faj,ascj->fsca', masked_rows, trig_tab, precision=lax.Precision.HIGHEST)
    factor = valid_wave[:, :, None] * sign_pair / points.astype(jnp.float32)[:, None, None]
    return summed * jnp.transpose(factor, (1, 2, 0))[None]


def mix_levels(grid_rows, level_mix, grid_scale):
    fields, lats, lons = grid_rows.shape
    stacked = grid_rows.reshape(fields // NLEV, NLEV, lats, lons)
    mixed_grid = jnp.einsum('ik,bkaj->biaj', level_mix, stacked, precision=lax.Precision.HIGHEST)
    return mixed_grid.reshape(fields, lats, lons) * grid_scale[None]


def reference(spectral, legendre, slot_wave, lat_points, level_mix, grid_scale, gauss_w):
    degree = jnp.arange(M, dtype=jnp.int32)

    def inverse_slot(item):
        spec_slot, leg_slot, wave_slot = item
        masked = jnp.where(degree >= wave_slot, spec_slot.astype(jnp.float32), 0.0)
        return jnp.einsum('cfn,ln->cfl', masked, leg_slot.astype(jnp.float32)).astype(jnp.bfloat16)

    four_coef = lax.map(inverse_slot, (spectral, legendre, slot_wave))
    slot_of = jnp.zeros((M + 1,), jnp.int32).at[slot_wave].set(jnp.arange(SLOTS, dtype=jnp.int32))[:M]
    by_wave = jnp.take(four_coef, slot_of, axis=0)
    lat_major = jnp.moveaxis(by_wave, 3, 0)

    def per_latitude(item):
        coef_lat, points, scale_row = item
        grid_rows = inverse_terms(coef_lat[..., None], degree, points[None], 0, LONS)
        mixed_grid = mix_levels(grid_rows, level_mix, scale_row[None])
        back_coef = direct_terms(mixed_grid, degree, points[None], 0, LONS)
        return grid_rows[:, 0], back_coef[..., 0]

    grid_lat, back_lat = lax.map(per_latitude, (lat_major, lat_points, grid_scale))
    grid_out = jnp.moveaxis(grid_lat, 0, 1)
    fourier_back = lax.optimization_barrier(back_lat.astype(jnp.bfloat16))
    weighted = (fourier_back.astype(jnp.float32) * gauss_w[:, None, None, None]).astype(jnp.bfloat16)
    by_slot = jnp.take(weighted, jnp.minimum(slot_wave, M - 1), axis=2)

    def direct_slot(item):
        coef_slot, leg_slot, wave_slot = item
        summed = jnp.einsum('lfc,ln->cfn', coef_slot.astype(jnp.float32), leg_slot.astype(jnp.float32))
        return jnp.where(degree >= wave_slot, summed, 0.0).astype(jnp.bfloat16)

    spec_out = lax.map(direct_slot, (jnp.moveaxis(by_slot, 2, 0), legendre, slot_wave))
    return grid_out, spec_out
```

```python
import math

import jax
import jax.numpy as jnp
from jax import lax
from jax.experimental import pallas as pl
from jax.experimental.pallas import tpu as pltpu
from jax.sharding import PartitionSpec as P

TWO_PI = 2.0 * math.pi
VMEM_LIMIT = 56 * 1024 * 1024
NT = (((1,), (1,)), ((), ()))
NN = (((1,), (0,)), ((), ()))


def dot(a, b, dims):
    return lax.dot_general(a, b, dims, preferred_element_type=jnp.float32)


def masked_legendre(leg_ref, thr_ref):
    rows, degrees = leg_ref.shape
    degree = lax.broadcasted_iota(jnp.int32, (rows, degrees), 1)
    keep = degree >= thr_ref[...][:, :1]
    return jnp.where(keep, leg_ref[...].astype(jnp.float32), 0.0).astype(jnp.bfloat16)


def forward_kernel(lats, spec_ref, leg_ref, thr_ref, out_ref):
    slots, pairs, degrees = spec_ref.shape
    legm = masked_legendre(leg_ref, thr_ref)
    lane_slot = lax.broadcasted_iota(jnp.int32, (pairs, slots * lats), 1) // lats
    total = jnp.zeros((pairs, slots * lats), jnp.float32)
    step = 4
    for first in range(0, slots, step):
        block = spec_ref[first : first + step].reshape(step * pairs, degrees)
        res = dot(block, legm, NT)
        for k in range(step):
            total = jnp.where(lane_slot == first + k, res[k * pairs : (k + 1) * pairs], total)
    out_ref[...] = total.astype(jnp.bfloat16)


def backward_kernel(lats, coef_ref, leg_ref, thr_ref, out_ref):
    slots, pairs, degrees = out_ref.shape
    legm = masked_legendre(leg_ref, thr_ref)
    lane_slot = lax.broadcasted_iota(jnp.int32, (pairs, slots * lats), 1) // lats
    coef = coef_ref[...].astype(jnp.float32)
    step = 4
    for first in range(0, slots, step):
        lhs = jnp.concatenate(
            [jnp.where(lane_slot == first + k, coef, 0.0) for k in range(step)], axis=0
        ).astype(jnp.bfloat16)
        res = dot(lhs, legm, NN).astype(jnp.bfloat16)
        out_ref[first : first + step] = res.reshape(step, pairs, degrees)


def turn(product, points, inverse):
    whole = jnp.round(product * inverse)
    x = (product - whole * points) * inverse * TWO_PI
    y = x * x
    c = 1.0
    for k in range(9, 0, -1):
        c = 1.0 - c * y * (1.0 / ((2 * k - 1) * (2 * k)))
    s = 1.0
    for k in range(9, 0, -1):
        s = 1.0 - s * y * (1.0 / ((2 * k) * (2 * k + 1)))
    return c, s * x


def table_kernel(lanes, wave_ref, points_ref, out_ref):
    rows = out_ref.shape[0]
    slots = wave_ref.shape[1]
    points = points_ref[0].astype(jnp.float32)
    inverse = 1.0 / jnp.full((1, 1), points, jnp.float32)
    for start in range(0, slots, lanes):
        here = pl.ds(start, lanes)
        there = pl.ds(slots + start, lanes)
        wave = wave_ref[:, here].astype(jnp.float32)
        lon = lax.broadcasted_iota(jnp.int32, (16, lanes), 0).astype(jnp.float32)
        c0, s0 = turn(wave * lon, points, inverse)
        cr, sr = turn(jnp.broadcast_to(wave, (8, lanes)) * 16.0, points, inverse)
        cr = jnp.concatenate([cr, cr], axis=0)
        sr = jnp.concatenate([sr, sr], axis=0)

        def step(i, held):
            c, s = held
            at = pl.ds(pl.multiple_of(i * 16, 16), 16)
            out_ref[at, here] = c.astype(jnp.bfloat16)
            out_ref[at, there] = s.astype(jnp.bfloat16)
            return c * cr - s * sr, s * cr + c * sr

        lax.fori_loop(0, rows // 16, step, (c0, s0), unroll=2)


def grid_kernel(
    levels, coef_ref, table_ref, wave_ref, points_ref, mix_ref, scale_ref,
    grid_ref, back_ref, canvas, groups, sums,
):
    fields = coef_ref.shape[0] // 2
    rows = table_ref.shape[0]
    slots = wave_ref.shape[1]
    lons = grid_ref.shape[1]
    points = points_ref[0]
    quarter = points // 4
    wave = wave_ref[...]
    rest = wave & 3
    valid = jnp.where(2 * wave < points, 1.0, 0.0)
    odd = (rest & 1).astype(jnp.float32)
    even = 1.0 - odd
    sign_even = even * (1.0 - rest.astype(jnp.float32))
    sign_odd = odd * (rest.astype(jnp.float32) - 2.0)
    factor = valid * jnp.where(wave == 0, 1.0, 2.0)
    a = coef_ref[:fields].astype(jnp.float32) * factor
    b = coef_ref[fields:].astype(jnp.float32) * factor
    low, high = pl.ds(0, slots), pl.ds(slots, slots)
    for k, (to_cos, to_sin) in enumerate(
        ((a * even, -b * even), (a * odd, -b * odd), (a * sign_even, -b * sign_even), (b * sign_odd, a * sign_odd))
    ):
        at = pl.ds(k * fields, fields)
        groups[at, low] = to_cos.astype(jnp.bfloat16)
        groups[at, high] = to_sin.astype(jnp.bfloat16)

    part = rows // 4

    @pl.loop(0, 4)
    def _(i):
        at = pl.ds(pl.multiple_of(i * part, 16), part)
        sums[at, :] = dot(table_ref[at, :], groups[...], NT)

    ga = sums[:, 0 * fields : 1 * fields]
    gb = sums[:, 1 * fields : 2 * fields]
    gc = sums[:, 2 * fields : 3 * fields]
    gd = sums[:, 3 * fields : 4 * fields]
    for r, x in enumerate((ga + gb, gc + gd, ga - gb, gc - gd)):
        canvas[pl.ds(r * quarter, rows), :] = x

    tile = 128

    @pl.loop(0, lons // tile)
    def _(i):
        at = pl.ds(pl.multiple_of(i * tile, tile), tile)
        lon = i * tile + lax.broadcasted_iota(jnp.int32, (tile, fields), 0)
        g = jnp.where(lon < points, canvas[at, :], 0.0)
        grid_ref[:, at] = g.T.astype(jnp.bfloat16)
        gl = g.astype(jnp.bfloat16)
        mixed = [
            dot(gl[:, f : f + levels], mix_ref[...], NT) for f in range(0, fields, levels)
        ]
        mixed = mixed[0] if len(mixed) == 1 else jnp.concatenate(mixed, axis=1)
        canvas[at, :] = mixed * scale_ref[at, :]

    inside = lax.broadcasted_iota(jnp.int32, (rows, fields), 0) < quarter
    y = [jnp.where(inside, canvas[pl.ds(r * quarter, rows), :], 0.0) for r in range(4)]
    p, q, v, w = y[0] + y[2], y[1] + y[3], y[0] - y[2], y[1] - y[3]
    sums[:, 0 * fields : 1 * fields] = p + q
    sums[:, 1 * fields : 2 * fields] = p - q
    sums[:, 2 * fields : 3 * fields] = v
    sums[:, 3 * fields : 4 * fields] = w
    u = sums[...].T.astype(jnp.bfloat16)
    over = 1.0 / jnp.full((1, 1), points.astype(jnp.float32), jnp.float32)
    width = 512 if slots % 512 == 0 else 128

    @pl.loop(0, slots // width)
    def _(i):
        at = pl.ds(pl.multiple_of(i * width, width), width)
        to = pl.ds(pl.multiple_of(slots + i * width, width), width)
        zc = dot(u, table_ref[:, at], NN)
        zs = dot(u, table_ref[:, to], NN)
        wv = wave_ref[:, at]
        rs = wv & 3
        gain = jnp.where(2 * wv < points, 1.0, 0.0) * over
        sg = jnp.where(rs == 1, -1.0, 1.0)
        f0, f1, f2, f3 = (slice(k * fields, (k + 1) * fields) for k in range(4))
        is0, is2 = rs == 0, rs == 2
        re = jnp.where(is0, zc[f0], jnp.where(is2, zc[f1], zc[f2] + sg * zs[f3]))
        im = jnp.where(is0, -zs[f0], jnp.where(is2, -zs[f1], sg * zc[f3] - zs[f2]))
        back_ref[0:fields, at] = (re * gain).astype(jnp.bfloat16)
        back_ref[fields : 2 * fields, at] = (im * gain).astype(jnp.bfloat16)


def params():
    return pltpu.CompilerParams(vmem_limit_bytes=VMEM_LIMIT)


def whole():
    return pl.BlockSpec(memory_space=pltpu.VMEM)


def scalar():
    return pl.BlockSpec(memory_space=pltpu.SMEM)


def make_table(wave_row, points, rows):
    slots = wave_row.shape[1]
    return pl.pallas_call(
        lambda *refs: table_kernel(512 if slots % 512 == 0 else 128, *refs),
        out_shape=jax.ShapeDtypeStruct((rows, 2 * slots), jnp.bfloat16),
        in_specs=[whole(), scalar()],
        out_specs=whole(),
        compiler_params=params(),
        cost_estimate=pl.CostEstimate(
            flops=16 * rows * slots, bytes_accessed=4 * rows * slots, transcendentals=0
        ),
        name="trig_table",
    )(wave_row, points)


def on_grid(levels, coef, table, wave_row, points, mix, scale_cols, lons):
    pairs, slots = coef.shape
    fields = pairs // 2
    rows = table.shape[0]
    return pl.pallas_call(
        lambda *refs: grid_kernel(levels, *refs),
        out_shape=(
            jax.ShapeDtypeStruct((fields, lons), jnp.bfloat16),
            jax.ShapeDtypeStruct((pairs, slots), jnp.bfloat16),
        ),
        in_specs=[whole(), whole(), whole(), scalar(), whole(), whole()],
        out_specs=(whole(), whole()),
        scratch_shapes=[
            pltpu.VMEM((lons + rows, fields), jnp.float32),
            pltpu.VMEM((4 * fields, 2 * slots), jnp.bfloat16),
            pltpu.VMEM((rows, 4 * fields), jnp.float32),
        ],
        compiler_params=params(),
        cost_estimate=pl.CostEstimate(
            flops=4 * rows * 2 * slots * 4 * fields,
            bytes_accessed=4 * rows * slots,
            transcendentals=0,
        ),
        name="grid_step",
    )(coef, table, wave_row, points, mix, scale_cols)


def block_slots(slots, lats):
    for count in (16, 8, 4):
        if slots % count == 0 and (count * lats) % 128 == 0:
            return count
    return 0


def body(spectral, legendre, slot_wave, lat_points, level_mix, grid_scale, gauss_w):
    slots, _, fields, degrees = spectral.shape
    lats = legendre.shape[1]
    levels = level_mix.shape[0]
    pairs = 2 * fields
    waves = slot_wave.shape[0] // slots
    bands = lax.axis_size("band")
    lon_width = grid_scale.shape[1]
    lons = lon_width * bands
    rows = -(-lons // 512) * 128
    wave_here = lax.dynamic_slice_in_dim(slot_wave, lax.axis_index("wave") * slots, slots)
    count = block_slots(slots, lats)
    empty = degrees

    padded = -(-slots // 128) * 128 if slots >= 128 else slots
    spread = jnp.pad(
        slot_wave.reshape(waves, slots), ((0, 0), (0, padded - slots)), constant_values=empty
    ).reshape(1, waves * padded)
    total = -(-(waves * padded) // 512) * 512
    wave_row = jnp.pad(spread, ((0, 0), (0, total - waves * padded)), constant_values=empty)
    wave_row = jnp.where(wave_row >= empty, 4 * lons, wave_row)
    table_wave = jnp.where(wave_row >= 4 * lons, 0, wave_row)
    scale_all = lax.all_gather(grid_scale, "band", axis=1, tiled=True)

    if count:
        thr = jnp.broadcast_to(wave_here[:, None, None], (slots, lats, 128)).reshape(-1, 128)
        leg_rows = legendre.reshape(slots * lats, degrees)
        block = count * lats
        legendre_cost = pl.CostEstimate(
            flops=2 * slots * pairs * degrees * block,
            bytes_accessed=2 * slots * (pairs + lats) * degrees,
            transcendentals=0,
        )
        leg_specs = [
            pl.BlockSpec((block, degrees), lambda i: (i, 0)),
            pl.BlockSpec((block, 128), lambda i: (i, 0)),
        ]
        coef = pl.pallas_call(
            lambda *refs: forward_kernel(lats, *refs),
            grid=(slots // count,),
            out_shape=jax.ShapeDtypeStruct((pairs, slots * lats), jnp.bfloat16),
            in_specs=[pl.BlockSpec((count, pairs, degrees), lambda i: (i, 0, 0))] + leg_specs,
            out_specs=pl.BlockSpec((pairs, block), lambda i: (0, i)),
            compiler_params=params(),
            cost_estimate=legendre_cost,
            name="legendre_forward",
        )(spectral.reshape(slots, pairs, degrees), leg_rows, thr)
        coef = jnp.transpose(coef.reshape(pairs, slots, lats), (2, 0, 1))
    else:
        keep = jnp.arange(degrees, dtype=jnp.int32)[None, :] >= wave_here[:, None]
        kept = jnp.where(keep[:, None, :], legendre, jnp.zeros((), jnp.bfloat16))
        coef = jnp.einsum(
            "spn,sln->lps",
            spectral.reshape(slots, pairs, degrees),
            kept,
            preferred_element_type=jnp.float32,
        ).astype(jnp.bfloat16)
    coef = jnp.pad(coef, ((0, 0), (0, 0), (0, padded - slots)))
    local = lats // waves
    coef = lax.all_to_all(
        coef.reshape(waves, local, pairs, padded), "wave", split_axis=0, concat_axis=0, tiled=True
    )

    mix = level_mix.astype(jnp.bfloat16)
    split = fields % levels != 0
    grid_parts, back_parts = [], []
    for lat in range(local):
        x = jnp.transpose(coef[:, lat], (1, 0, 2)).reshape(pairs, waves * padded)
        x = jnp.pad(x, ((0, 0), (0, total - waves * padded)))
        points = lat_points[lat : lat + 1]
        table = make_table(table_wave, points, rows)
        group = fields
        if split:
            x = lax.all_gather(x.reshape(2, fields, total), "band", axis=1, tiled=True)
            group = fields * bands
            x = x.reshape(2 * group, total)
        scale_cols = jnp.broadcast_to(scale_all[lat][:, None], (lons, group))
        g, back = on_grid(levels, x, table, wave_row, points, mix, scale_cols, lons)
        if split:
            mine = lax.axis_index("band") * fields
            g = lax.dynamic_slice_in_dim(g, mine, fields, axis=0)
            back = lax.dynamic_slice_in_dim(
                back.reshape(2, group, total), mine, fields, axis=1
            ).reshape(pairs, total)
        grid_parts.append(g.reshape(fields, bands, lon_width))
        back_parts.append(back[:, : waves * padded].reshape(pairs, waves, padded))
    back = jnp.stack([jnp.transpose(b, (1, 0, 2)) for b in back_parts], axis=1)
    back = lax.all_to_all(back, "wave", split_axis=0, concat_axis=0, tiled=True)
    back = back.reshape(lats, pairs, padded)[:, :, :slots]
    grid = jnp.stack(grid_parts, axis=2)
    back, grid = lax.optimization_barrier((back, grid))
    grid = lax.all_to_all(grid, "band", split_axis=1, concat_axis=0, tiled=True)
    grid_out = grid.reshape(fields * bands, local, lon_width).astype(jnp.float32)

    weighted = (back.astype(jnp.float32) * gauss_w[:, None, None]).astype(jnp.bfloat16)
    if count:
        coef = jnp.transpose(weighted, (1, 2, 0)).reshape(pairs, slots * lats)
        spec_out = pl.pallas_call(
            lambda *refs: backward_kernel(lats, *refs),
            grid=(slots // count,),
            out_shape=jax.ShapeDtypeStruct((slots, pairs, degrees), jnp.bfloat16),
            in_specs=[pl.BlockSpec((pairs, block), lambda i: (0, i))] + leg_specs,
            out_specs=pl.BlockSpec((count, pairs, degrees), lambda i: (i, 0, 0)),
            compiler_params=params(),
            cost_estimate=legendre_cost,
            name="legendre_backward",
        )(coef, leg_rows, thr)
    else:
        spec_out = jnp.einsum(
            "lps,sln->spn", weighted, kept, preferred_element_type=jnp.float32
        ).astype(jnp.bfloat16)
    return grid_out, spec_out.reshape(slots, 2, fields, degrees)


def solution(mesh):
    placed = (
        P("wave", None, "band", None),
        P("wave", None, None),
        P(),
        P("wave"),
        P(),
        P("wave", "band"),
        P(),
    )
    return jax.shard_map(
        body,
        mesh=mesh,
        in_specs=placed,
        out_specs=(P(None, "wave", "band"), P("wave", None, "band", None)),
        check_vma=False,
    )
```

```python
import math

import jax
import jax.numpy as jnp
from jax import lax
from jax.experimental import pallas as pl
from jax.experimental.pallas import tpu as pltpu
from jax.sharding import PartitionSpec as P

TWO_PI = 2.0 * math.pi
VMEM_LIMIT = 56 * 1024 * 1024
NT = (((1,), (1,)), ((), ()))
NN = (((1,), (0,)), ((), ()))


def dot(a, b, dims):
    return lax.dot_general(a, b, dims, preferred_element_type=jnp.float32)


def masked_legendre(leg_ref, thr_ref):
    rows, degrees = leg_ref.shape
    degree = lax.broadcasted_iota(jnp.int32, (rows, degrees), 1)
    keep = degree >= thr_ref[...][:, :1]
    return jnp.where(keep, leg_ref[...].astype(jnp.float32), 0.0).astype(jnp.bfloat16)


def forward_kernel(lats, spec_ref, leg_ref, thr_ref, out_ref):
    slots, pairs, degrees = spec_ref.shape
    legm = masked_legendre(leg_ref, thr_ref)
    lane_slot = lax.broadcasted_iota(jnp.int32, (pairs, slots * lats), 1) // lats
    total = jnp.zeros((pairs, slots * lats), jnp.float32)
    step = slots
    for first in range(0, slots, step):
        block = spec_ref[first : first + step].reshape(step * pairs, degrees)
        res = dot(block, legm, NT)
        for k in range(step):
            total = jnp.where(lane_slot == first + k, res[k * pairs : (k + 1) * pairs], total)
    out_ref[...] = total.astype(jnp.bfloat16)


def backward_kernel(lats, coef_ref, leg_ref, thr_ref, out_ref):
    slots, pairs, degrees = out_ref.shape
    legm = masked_legendre(leg_ref, thr_ref)
    lane_slot = lax.broadcasted_iota(jnp.int32, (pairs, slots * lats), 1) // lats
    coef = coef_ref[...].astype(jnp.float32)
    lhs = jnp.concatenate(
        [jnp.where(lane_slot == k, coef, 0.0) for k in range(slots)], axis=0
    ).astype(jnp.bfloat16)
    width = 256 if degrees % 256 == 0 else degrees
    for first in range(0, degrees, width):
        res = dot(lhs, legm[:, first : first + width], NN).astype(jnp.bfloat16)
        out_ref[:, :, first : first + width] = res.reshape(slots, pairs, width)


def turn(product, points, inverse):
    whole = jnp.round(product * inverse)
    x = (product - whole * points) * inverse * TWO_PI
    y = x * x
    c = 1.0
    for k in range(9, 0, -1):
        c = 1.0 - c * y * (1.0 / ((2 * k - 1) * (2 * k)))
    s = 1.0
    for k in range(9, 0, -1):
        s = 1.0 - s * y * (1.0 / ((2 * k) * (2 * k + 1)))
    return c, s * x


def table_kernel(lanes, wave_ref, points_ref, out_ref):
    rows = out_ref.shape[0]
    slots = wave_ref.shape[1]
    points = points_ref[0].astype(jnp.float32)
    inverse = 1.0 / jnp.full((1, 1), points, jnp.float32)
    for start in range(0, slots, lanes):
        here = pl.ds(start, lanes)
        there = pl.ds(slots + start, lanes)
        wave = wave_ref[:, here].astype(jnp.float32)
        lon = lax.broadcasted_iota(jnp.int32, (16, lanes), 0).astype(jnp.float32)
        c0, s0 = turn(wave * lon, points, inverse)
        cr, sr = turn(jnp.broadcast_to(wave, (8, lanes)) * 16.0, points, inverse)
        cr = jnp.concatenate([cr, cr], axis=0)
        sr = jnp.concatenate([sr, sr], axis=0)

        def step(i, held):
            c, s = held
            at = pl.ds(pl.multiple_of(i * 16, 16), 16)
            out_ref[at, here] = c.astype(jnp.bfloat16)
            out_ref[at, there] = s.astype(jnp.bfloat16)
            return c * cr - s * sr, s * cr + c * sr

        lax.fori_loop(0, rows // 16, step, (c0, s0), unroll=2)


def grid_kernel(
    levels, coef_ref, table_hbm, wave_ref, points_ref, mix_ref, scale_ref,
    grid_ref, back_ref, canvas, groups, sums, table_ref, arrived,
):
    fields = coef_ref.shape[0] // 2
    rows = table_ref.shape[0]
    slots = wave_ref.shape[1]
    lons = grid_ref.shape[1]
    part = rows // 4
    copies = [
        pltpu.make_async_copy(
            table_hbm.at[pl.ds(i * part, part)],
            table_ref.at[pl.ds(i * part, part)],
            arrived.at[i],
        )
        for i in range(4)
    ]
    for copy in copies:
        copy.start()
    points = points_ref[0]
    quarter = points // 4
    wave = wave_ref[...]
    rest = wave & 3
    valid = jnp.where(2 * wave < points, 1.0, 0.0)
    odd = (rest & 1).astype(jnp.float32)
    even = 1.0 - odd
    sign_even = even * (1.0 - rest.astype(jnp.float32))
    sign_odd = odd * (rest.astype(jnp.float32) - 2.0)
    factor = valid * jnp.where(wave == 0, 1.0, 2.0)
    a = coef_ref[:fields].astype(jnp.float32) * factor
    b = coef_ref[fields:].astype(jnp.float32) * factor
    low, high = pl.ds(0, slots), pl.ds(slots, slots)
    for k, (to_cos, to_sin) in enumerate(
        ((a * even, -b * even), (a * odd, -b * odd), (a * sign_even, -b * sign_even), (b * sign_odd, a * sign_odd))
    ):
        at = pl.ds(k * fields, fields)
        groups[at, low] = to_cos.astype(jnp.bfloat16)
        groups[at, high] = to_sin.astype(jnp.bfloat16)

    for i in range(4):
        copies[i].wait()
        at = pl.ds(i * part, part)
        sums[at, :] = dot(table_ref[at, :], groups[...], NT)

    ga = sums[:, 0 * fields : 1 * fields]
    gb = sums[:, 1 * fields : 2 * fields]
    gc = sums[:, 2 * fields : 3 * fields]
    gd = sums[:, 3 * fields : 4 * fields]
    for r, x in enumerate((ga + gb, gc + gd, ga - gb, gc - gd)):
        canvas[pl.ds(r * quarter, rows), :] = x

    tile = 512 if lons % 512 == 0 else 128

    @pl.loop(0, lons // tile)
    def _(i):
        at = pl.ds(pl.multiple_of(i * tile, tile), tile)
        lon = i * tile + lax.broadcasted_iota(jnp.int32, (tile, fields), 0)
        g = jnp.where(lon < points, canvas[at, :], 0.0)
        grid_ref[:, at] = g.T.astype(jnp.bfloat16)
        gl = g.astype(jnp.bfloat16)
        mixed = [
            dot(gl[:, f : f + levels], mix_ref[...], NT) for f in range(0, fields, levels)
        ]
        mixed = mixed[0] if len(mixed) == 1 else jnp.concatenate(mixed, axis=1)
        canvas[at, :] = mixed * jnp.broadcast_to(scale_ref[:, at], (fields, tile)).T

    inside = lax.broadcasted_iota(jnp.int32, (rows, fields), 0) < quarter
    y = [jnp.where(inside, canvas[pl.ds(r * quarter, rows), :], 0.0) for r in range(4)]
    p, q, v, w = y[0] + y[2], y[1] + y[3], y[0] - y[2], y[1] - y[3]
    sums[:, 0 * fields : 1 * fields] = p + q
    sums[:, 1 * fields : 2 * fields] = p - q
    sums[:, 2 * fields : 3 * fields] = v
    sums[:, 3 * fields : 4 * fields] = w
    u = sums[...].T.astype(jnp.bfloat16)
    over = 1.0 / jnp.full((1, 1), points.astype(jnp.float32), jnp.float32)
    width = 512 if slots % 512 == 0 else 128

    @pl.loop(0, slots // width)
    def _(i):
        at = pl.ds(pl.multiple_of(i * width, width), width)
        to = pl.ds(pl.multiple_of(slots + i * width, width), width)
        zc = dot(u, table_ref[:, at], NN)
        zs = dot(u, table_ref[:, to], NN)
        wv = wave_ref[:, at]
        rs = wv & 3
        gain = jnp.where(2 * wv < points, 1.0, 0.0) * over
        sg = jnp.where(rs == 1, -1.0, 1.0)
        f0, f1, f2, f3 = (slice(k * fields, (k + 1) * fields) for k in range(4))
        is0, is2 = rs == 0, rs == 2
        re = jnp.where(is0, zc[f0], jnp.where(is2, zc[f1], zc[f2] + sg * zs[f3]))
        im = jnp.where(is0, -zs[f0], jnp.where(is2, -zs[f1], sg * zc[f3] - zs[f2]))
        back_ref[0:fields, at] = (re * gain).astype(jnp.bfloat16)
        back_ref[fields : 2 * fields, at] = (im * gain).astype(jnp.bfloat16)


def params():
    return pltpu.CompilerParams(vmem_limit_bytes=VMEM_LIMIT)


def whole():
    return pl.BlockSpec(memory_space=pltpu.VMEM)


def scalar():
    return pl.BlockSpec(memory_space=pltpu.SMEM)


def make_table(wave_row, points, rows):
    slots = wave_row.shape[1]
    return pl.pallas_call(
        lambda *refs: table_kernel(512 if slots % 512 == 0 else 128, *refs),
        out_shape=jax.ShapeDtypeStruct((rows, 2 * slots), jnp.bfloat16),
        in_specs=[whole(), scalar()],
        out_specs=whole(),
        compiler_params=params(),
        cost_estimate=pl.CostEstimate(
            flops=16 * rows * slots, bytes_accessed=4 * rows * slots, transcendentals=0
        ),
        name="trig_table",
    )(wave_row, points)


def on_grid(levels, coef, table, wave_row, points, mix, scale_row, lons):
    pairs, slots = coef.shape
    fields = pairs // 2
    rows = table.shape[0]
    return pl.pallas_call(
        lambda *refs: grid_kernel(levels, *refs),
        out_shape=(
            jax.ShapeDtypeStruct((fields, lons), jnp.bfloat16),
            jax.ShapeDtypeStruct((pairs, slots), jnp.bfloat16),
        ),
        in_specs=[
            whole(), pl.BlockSpec(memory_space=pl.ANY), whole(), scalar(), whole(), whole()
        ],
        out_specs=(whole(), whole()),
        scratch_shapes=[
            pltpu.VMEM((lons + rows, fields), jnp.float32),
            pltpu.VMEM((4 * fields, 2 * slots), jnp.bfloat16),
            pltpu.VMEM((rows, 4 * fields), jnp.float32),
            pltpu.VMEM((rows, 2 * slots), jnp.bfloat16),
            pltpu.SemaphoreType.DMA((4,)),
        ],
        compiler_params=params(),
        cost_estimate=pl.CostEstimate(
            flops=4 * rows * 2 * slots * 4 * fields,
            bytes_accessed=4 * rows * slots,
            transcendentals=0,
        ),
        name="grid_step",
    )(coef, table, wave_row, points, mix, scale_row)


def gather_rows(x, bands):
    me = lax.axis_index("band")
    parts = [x]
    for k in range(1, bands):
        parts.append(lax.ppermute(x, "band", [((d + k) % bands, d) for d in range(bands)]))
    turned = jnp.concatenate(parts + parts, axis=1)
    start = lax.rem(bands - me, bands) * x.shape[1]
    return lax.dynamic_slice_in_dim(turned, start, bands * x.shape[1], axis=1)


def block_slots(slots, lats):
    for count in (16, 8, 4):
        if slots % count == 0 and (count * lats) % 128 == 0:
            return count
    return 0


def body(spectral, legendre, slot_wave, lat_points, level_mix, grid_scale, gauss_w):
    slots, _, fields, degrees = spectral.shape
    lats = legendre.shape[1]
    levels = level_mix.shape[0]
    pairs = 2 * fields
    waves = slot_wave.shape[0] // slots
    bands = lax.axis_size("band")
    lon_width = grid_scale.shape[1]
    lons = lon_width * bands
    rows = -(-lons // 512) * 128
    wave_here = lax.dynamic_slice_in_dim(slot_wave, lax.axis_index("wave") * slots, slots)
    count = block_slots(slots, lats)
    empty = degrees

    padded = -(-slots // 128) * 128 if slots >= 128 else slots
    spread = jnp.pad(
        slot_wave.reshape(waves, slots), ((0, 0), (0, padded - slots)), constant_values=empty
    ).reshape(1, waves * padded)
    total = -(-(waves * padded) // 512) * 512
    wave_row = jnp.pad(spread, ((0, 0), (0, total - waves * padded)), constant_values=empty)
    wave_row = jnp.where(wave_row >= empty, 4 * lons, wave_row)
    table_wave = jnp.where(wave_row >= 4 * lons, 0, wave_row)
    scale_all = gather_rows(grid_scale, bands)

    if count:
        thr = jnp.broadcast_to(wave_here[:, None, None], (slots, lats, 128)).reshape(-1, 128)
        leg_rows = legendre.reshape(slots * lats, degrees)
        block = count * lats
        legendre_cost = pl.CostEstimate(
            flops=2 * slots * pairs * degrees * block,
            bytes_accessed=2 * slots * (pairs + lats) * degrees,
            transcendentals=0,
        )
        leg_specs = [
            pl.BlockSpec((block, degrees), lambda i: (i, 0)),
            pl.BlockSpec((block, 128), lambda i: (i, 0)),
        ]
        coef = pl.pallas_call(
            lambda *refs: forward_kernel(lats, *refs),
            grid=(slots // count,),
            out_shape=jax.ShapeDtypeStruct((pairs, slots * lats), jnp.bfloat16),
            in_specs=[pl.BlockSpec((count, pairs, degrees), lambda i: (i, 0, 0))] + leg_specs,
            out_specs=pl.BlockSpec((pairs, block), lambda i: (0, i)),
            compiler_params=params(),
            cost_estimate=legendre_cost,
            name="legendre_forward",
        )(spectral.reshape(slots, pairs, degrees), leg_rows, thr)
        coef = jnp.transpose(coef.reshape(pairs, slots, lats), (2, 0, 1))
    else:
        keep = jnp.arange(degrees, dtype=jnp.int32)[None, :] >= wave_here[:, None]
        kept = jnp.where(keep[:, None, :], legendre, jnp.zeros((), jnp.bfloat16))
        coef = jnp.einsum(
            "spn,sln->lps",
            spectral.reshape(slots, pairs, degrees),
            kept,
            preferred_element_type=jnp.float32,
        ).astype(jnp.bfloat16)
    coef = jnp.pad(coef, ((0, 0), (0, 0), (0, padded - slots)))
    local = lats // waves
    coef = lax.all_to_all(
        coef.reshape(waves, local, pairs, padded), "wave", split_axis=0, concat_axis=0, tiled=True
    )

    mix = level_mix.astype(jnp.bfloat16)
    split = fields % levels != 0
    grid_parts, back_parts = [], []
    for lat in range(local):
        x = jnp.transpose(coef[:, lat], (1, 0, 2)).reshape(pairs, waves * padded)
        x = jnp.pad(x, ((0, 0), (0, total - waves * padded)))
        points = lat_points[lat : lat + 1]
        table = make_table(table_wave, points, rows)
        group = fields
        if split:
            x = lax.all_gather(x.reshape(2, fields, total), "band", axis=1, tiled=True)
            group = fields * bands
            x = x.reshape(2 * group, total)
        g, back = on_grid(levels, x, table, wave_row, points, mix, scale_all[lat : lat + 1], lons)
        if split:
            mine = lax.axis_index("band") * fields
            g = lax.dynamic_slice_in_dim(g, mine, fields, axis=0)
            back = lax.dynamic_slice_in_dim(
                back.reshape(2, group, total), mine, fields, axis=1
            ).reshape(pairs, total)
        grid_parts.append(g.reshape(fields, bands, lon_width))
        back_parts.append(back[:, : waves * padded].reshape(pairs, waves, padded))
    back = jnp.stack([jnp.transpose(b, (1, 0, 2)) for b in back_parts], axis=1)
    back = lax.all_to_all(back, "wave", split_axis=0, concat_axis=0, tiled=True)
    back = back.reshape(lats, pairs, padded)[:, :, :slots]
    grid = jnp.stack(grid_parts, axis=2)
    back, grid = lax.optimization_barrier((back, grid))
    grid = lax.all_to_all(grid, "band", split_axis=1, concat_axis=0, tiled=True)
    grid_out = grid.reshape(fields * bands, local, lon_width).astype(jnp.float32)

    weighted = (back.astype(jnp.float32) * gauss_w[:, None, None]).astype(jnp.bfloat16)
    if count:
        coef = jnp.transpose(weighted, (1, 2, 0)).reshape(pairs, slots * lats)
        spec_out = pl.pallas_call(
            lambda *refs: backward_kernel(lats, *refs),
            grid=(slots // count,),
            out_shape=jax.ShapeDtypeStruct((slots, pairs, degrees), jnp.bfloat16),
            in_specs=[pl.BlockSpec((pairs, block), lambda i: (0, i))] + leg_specs,
            out_specs=pl.BlockSpec((count, pairs, degrees), lambda i: (i, 0, 0)),
            compiler_params=params(),
            cost_estimate=legendre_cost,
            name="legendre_backward",
        )(coef, leg_rows, thr)
    else:
        spec_out = jnp.einsum(
            "lps,sln->spn", weighted, kept, preferred_element_type=jnp.float32
        ).astype(jnp.bfloat16)
    return grid_out, spec_out.reshape(slots, 2, fields, degrees)


def solution(mesh):
    placed = (
        P("wave", None, "band", None),
        P("wave", None, None),
        P(),
        P("wave"),
        P(),
        P("wave", "band"),
        P(),
    )
    return jax.shard_map(
        body,
        mesh=mesh,
        in_specs=placed,
        out_specs=(P(None, "wave", "band"), P("wave", None, "band", None)),
        check_vma=False,
    )
```
